512 devices in a mesh: section: 32 (over z_lo, y), dp: 16 (over z_hi, x, core).
Axes of the slice: x: 4, y: 4, z: 16 (z_hi: 2, z_lo: 8; z = z_hi * 8 + z_lo), core: 2. Of those that a mesh axis runs over, the one named last changes fastest.
Arguments:
- section_inputs: bfloat16 [32, 12, 1536, 512], P('section', None, 'dp'), may hold values from -6 to 6
- cotangent: bfloat16 [12, 1536, 512], P(None, 'dp'), may hold values from -6 to 6
- weight_in: bfloat16 [32, 512, 512], P('section', 'dp'), may hold values from -0.25 to 0.25
- weight_out: bfloat16 [32, 512, 512], P('section', 'dp'), may hold values from -0.25 to 0.25
Outputs:
- grad_in: float32 [32, 512, 512], P('section', 'dp')
- grad_out: float32 [32, 512, 512], P('section', 'dp')
- input_grad: bfloat16 [32, 12, 1536, 512], P('section', None, 'dp')
The draws below stay inside these ranges and needn't reach their ends.
All inputs are finite; a program needn't handle non-finite values.
Results may differ from the reference program's by a relative error of at most 0.029.
Values may be sent and summed in bfloat16 or wider, within the bound.
No kernel may reach another device: no remote copies, remote signals or barrier semaphores. Data moves between devices by JAX's collectives and lax.ppermute only.
A program may use at most 64 MiB of HBM per device.

```python
import jax
import jax.numpy as jnp
from jax import lax

C = 512
MICRO = 12
TOKENS = 1536
N_SECTION = 32


def steps_of(key, shape, pieces, low, high):
    def one(position, parts):
        draws = jax.random.uniform(jax.random.fold_in(jax.random.fold_in(key, 6), position), (parts,), jnp.float32, low / len(pieces), high / len(pieces))
        return jnp.repeat(jnp.exp(draws), shape[position] // parts).reshape((-1,) + (1,) * (len(shape) - position - 1))

    factor_of = one(*pieces[0])
    for cut in pieces[1:]:
        factor_of = factor_of * one(*cut)
    return factor_of


def gaussian(own_key, shape, width, bound, split=(), dtype=jnp.bfloat16):
    entries = width * jax.random.normal(own_key, shape, jnp.float32)
    if split:
        entries = entries * steps_of(own_key, shape, split, -0.22, 0.18)
    return jnp.clip(entries, -bound, bound).astype(dtype)


def setup_inputs(seed: int = 0) -> dict:
    seeds = jax.random.split(jax.random.key(seed), 5)
    section_inputs = gaussian(seeds[0], (N_SECTION, MICRO, TOKENS, C), 1.0, 6.0, ((0, 32), (2, 16)))
    cotangent = gaussian(seeds[1], (MICRO, TOKENS, C), 1.0, 6.0, ((1, 16),))
    weight_in = gaussian(seeds[2], (N_SECTION, C, C), C ** -0.5, 0.25, ((0, 32), (1, 16)))
    weight_out = gaussian(seeds[3], (N_SECTION, C, C), C ** -0.5, 0.25, ((0, 32), (1, 16)))
    return {"section_inputs": section_inputs, "cotangent": cotangent, "weight_in": weight_in, "weight_out": weight_out}


RHO = 0.25

def contract_rows(left, right):
    return lax.dot_general(left, right, (((0,), (0,)), ((), ())), preferred_element_type=jnp.float32)

def contract_cols(left, right):
    return lax.dot_general(left, right, (((1,), (1,)), ((), ())), preferred_element_type=jnp.float32)

def one_group(incoming, packed):
    inputs, w_in, w_out = packed

    def one_micro(sums, pair):
        grad_a, grad_b = sums
        x, g = pair
        z = jnp.dot(x, w_in, preferred_element_type=jnp.float32)
        h = jax.nn.silu(z).astype(jnp.bfloat16)
        sig = jax.nn.sigmoid(z)
        dz = (RHO * contract_cols(g, w_out) * sig * (1.0 + z * (1.0 - sig))).astype(jnp.bfloat16)
        dx = (g.astype(jnp.float32) + contract_cols(dz, w_in)).astype(jnp.bfloat16)
        grad_a = grad_a + contract_rows(x, dz)
        grad_b = grad_b + RHO * contract_rows(h, g)
        return ((grad_a, grad_b), dx)
    zeros = jnp.zeros((C, C), jnp.float32)
    sums, outgoing = lax.scan(one_micro, (zeros, zeros), (inputs, incoming))
    return (outgoing, (sums[0], sums[1], outgoing))

def reference(section_inputs, cotangent, weight_in, weight_out):
    final, outs = lax.scan(one_group, cotangent, (section_inputs, weight_in, weight_out), reverse=True)
    grad_a, grad_b, input_grad = outs
    factor = 4.0 / jnp.sqrt(jnp.float32(MICRO * TOKENS))
    return (grad_a * factor, grad_b * factor, input_grad)
```

```python
import jax
import jax.numpy as jnp
from jax import lax
from jax.sharding import PartitionSpec as P

RHO = 0.25
NY = 4
NZ = 8
NX = 4


def section_route(step_z, step_y):
    route = []
    for z in range(NZ):
        for y in range(NY):
            to_z = z + step_z
            if 0 <= to_z < NZ:
                route.append((z * NY + y, to_z * NY + (y + step_y) % NY))
    return route


def stage_route(source_z):
    return [(source_z * NY + y, (source_z - 1) * NY + y) for y in range(NY)]


def replica_route(step_zh, step_x, step_core):
    route = []
    for zh in range(2):
        for x in range(NX):
            for core in range(2):
                to = ((zh + step_zh) % 2, (x + step_x) % NX, (core + step_core) % 2)
                route.append(((zh * NX + x) * 2 + core, (to[0] * NX + to[1]) * 2 + to[2]))
    return route


def pick(array, index, axis):
    return lax.dynamic_index_in_dim(array, index, axis, keepdims=False)


def put(array, piece, index, axis):
    return lax.dynamic_update_index_in_dim(array, piece, index, axis)


def dot(left, right, left_dim, right_dim):
    return lax.dot_general(
        left, right, (((left_dim,), (right_dim,)), ((), ())), preferred_element_type=jnp.float32
    )


def slope(z):
    sig = jax.nn.sigmoid(z)
    return RHO * sig * (1.0 + z * (1.0 - sig))


def gather_weights(weight_in, weight_out, y, zh, x, core):
    own = jnp.concatenate([weight_in, weight_out], axis=0)
    rows, width = own.shape[1:]
    other = lax.ppermute(own, "dp", replica_route(1, 0, 0))
    both = put(jnp.stack([other, other]), own, zh, 0)
    sections = jnp.zeros((NY, 2, 2, rows, width), own.dtype)
    for step in range(NY):
        piece = both if step == 0 else lax.ppermute(both, "section", section_route(0, step))
        sections = put(sections, piece, (y - step) % NY, 0)
    along_x = jnp.zeros((NY, 2, 2, NX, rows, width), own.dtype)
    for step in range(NX):
        piece = sections if step == 0 else lax.ppermute(sections, "dp", replica_route(0, step, 0))
        along_x = put(along_x, piece, (x - step) % NX, 3)
    other = lax.ppermute(along_x, "dp", replica_route(0, 0, 1))
    full = put(jnp.stack([other, other], axis=4), along_x, core, 4)
    full = full.transpose(0, 2, 1, 3, 4, 5, 6)
    return full.reshape(NY, 2, 2 * NX * 2 * rows, width)


def exchange_rows(home, y):
    out = jnp.zeros_like(home)
    for step in range(NY):
        piece = pick(home, (y + step) % NY, 0)
        if step:
            piece = lax.ppermute(piece, "section", section_route(0, step))
        out = put(out, piece, (y - step) % NY, 0)
    return out


def reduce_replicas(grads, zh, x, core):
    width = grads.shape[-1]
    rows = grads.shape[1] // (2 * NX * 2)
    parts = grads.reshape(2, 2, NX, 2, rows, width)
    sent = pick(parts, 1 - core, 3).astype(jnp.bfloat16)
    total = pick(parts, core, 3) + lax.ppermute(sent, "dp", replica_route(0, 0, 1))
    acc = pick(total, x, 2)
    for step in range(1, NX):
        sent = pick(total, (x + step) % NX, 2).astype(jnp.bfloat16)
        acc = acc + lax.ppermute(sent, "dp", replica_route(0, step, 0))
    sent = pick(acc, 1 - zh, 1).astype(jnp.bfloat16)
    return pick(acc, zh, 1) + lax.ppermute(sent, "dp", replica_route(1, 0, 0))


def body(section_inputs, cotangent, weight_in, weight_out):
    position = lax.axis_index("section")
    replica = lax.axis_index("dp")
    z_stage, y = position // NY, position % NY
    zh, x, core = replica // (2 * NX), (replica // 2) % NX, replica % 2
    micro, rows, width = section_inputs.shape[1:]
    share = micro * rows // NY
    home_x = section_inputs[0].reshape(NY, share, width)

    weights = gather_weights(weight_in, weight_out, y, zh, x, core)
    stage_x = exchange_rows(home_x, y)
    slopes = [slope(dot(stage_x[s], weights[s, 0], 1, 0)) for s in range(NY)]

    given = pick(cotangent.reshape(NY, share, width), y, 0)
    g = jnp.where(z_stage == NZ - 1, given, jnp.zeros_like(given))
    kept = jnp.zeros((NY, share, width), jnp.bfloat16)
    for tick in range(NZ):
        active = z_stage == NZ - 1 - tick
        chain = [g]
        for s in reversed(range(0 if tick < NZ - 1 else 1, NY)):
            now = chain[-1]
            dz = (dot(now, weights[s, 1], 1, 1) * slopes[s]).astype(jnp.bfloat16)
            chain.append((now.astype(jnp.float32) + dot(dz, weights[s, 0], 1, 1)).astype(jnp.bfloat16))
        kept = jnp.where(active, jnp.stack(chain[NY - 1 :: -1]), kept)
        if tick < NZ - 1:
            g = lax.ppermute(chain[NY], "section", stage_route(NZ - 1 - tick))

    home_g = exchange_rows(kept, y).reshape(micro * rows, width)
    w_in, w_out = pick(weights[:, 0], y, 0), pick(weights[:, 1], y, 0)
    flat_x = section_inputs[0].reshape(micro * rows, width)
    flat_x, w_in, w_out, kept = lax.optimization_barrier((flat_x, w_in, w_out, kept))
    zed = dot(flat_x, w_in, 1, 0)
    h = jax.nn.silu(zed).astype(jnp.bfloat16)
    dz = (dot(home_g, w_out, 1, 1) * slope(zed)).astype(jnp.bfloat16)
    dx = (home_g.astype(jnp.float32) + dot(dz, w_in, 1, 1)).astype(jnp.bfloat16)
    grads = jnp.stack([dot(flat_x, dz, 0, 0), RHO * dot(h, home_g, 0, 0)])
    reduced = reduce_replicas(grads, zh, x, core)
    factor = 4.0 / jnp.sqrt(jnp.float32(micro * rows * lax.axis_size("dp")))
    reduced = reduced * factor
    return (reduced[0:1], reduced[1:2], dx.reshape(1, micro, rows, width))


def solution(mesh):
    return jax.shard_map(
        body,
        mesh=mesh,
        in_specs=(
            P("section", None, "dp", None),
            P(None, "dp", None),
            P("section", "dp", None),
            P("section", "dp", None),
        ),
        out_specs=(
            P("section", "dp", None),
            P("section", "dp", None),
            P("section", None, "dp", None),
        ),
        check_vma=False,
    )
```

```python
import functools

import jax
import jax.numpy as jnp
from jax import lax
from jax.experimental import pallas as pl
from jax.experimental.pallas import tpu as pltpu
from jax.sharding import PartitionSpec as P

RHO = 0.25
NY = 4
NZ = 8
NX = 4
VMEM_LIMIT = 32 * 1024 * 1024


def stage_route(source_z):
    return [(source_z * NY + y, (source_z - 1) * NY + y) for y in range(NY)]


def replica_route(step_zh, step_core):
    route = []
    for zh in range(2):
        for x in range(NX):
            for core in range(2):
                to = ((zh + step_zh) % 2, (core + step_core) % 2)
                route.append(((zh * NX + x) * 2 + core, (to[0] * NX + x) * 2 + to[1]))
    return route


def over_y(pieces):
    groups = [[z * NY + y for y in range(NY)] for z in range(NZ)]
    return lax.all_to_all(pieces, "section", 0, 0, axis_index_groups=groups)


def over_x(pieces):
    groups = [
        [(zh * NX + x) * 2 + core for x in range(NX)] for zh in range(2) for core in range(2)
    ]
    return lax.all_to_all(pieces, "dp", 0, 0, axis_index_groups=groups)


def dot(left, right, left_dim, right_dim):
    return lax.dot_general(
        left, right, (((left_dim,), (right_dim,)), ((), ())), preferred_element_type=jnp.float32
    )


def slope(z):
    sig = 1.0 / (1.0 + jnp.exp(-z))
    return RHO * sig * (1.0 + z * (1.0 - sig))


def call(kernel, out_shape, *operands, flops=0):
    whole = pl.BlockSpec(memory_space=pltpu.VMEM)
    specs = [
        pl.BlockSpec(memory_space=pltpu.SMEM) if o.dtype == jnp.int32 else whole for o in operands
    ]
    return pl.pallas_call(
        kernel,
        out_shape=out_shape,
        in_specs=specs,
        out_specs=jax.tree.map(lambda _: whole, out_shape),
        cost_estimate=pl.CostEstimate(flops=flops, bytes_accessed=0, transcendentals=0),
        compiler_params=pltpu.CompilerParams(vmem_limit_bytes=VMEM_LIMIT),
    )(*operands)


def prepare_kernel(lead, place, mine, other, arrived, weights, slopes):
    rows = mine.shape[4]
    own_at = place[1] * rows
    other_at = rows - own_at
    for s in reversed(range(NY)):
        for w in range(2):
            for zh in range(2):
                for x in range(NX):
                    base = (zh * NX + x) * 2 * rows
                    weights[s, w, pl.ds(pl.multiple_of(base + own_at, rows), rows)] = mine[x, s, zh, w]
                    weights[s, w, pl.ds(pl.multiple_of(base + other_at, rows), rows)] = other[x, s, zh, w]
        slopes[s] = slope(dot(arrived[s, lead:], weights[s, 0], 1, 0))


def stage_kernel(tick, place, arriving, weights, slopes, kept_in, kept, sending):
    last = tick == NZ - 1

    @pl.when(place[0] == NZ - 1 - tick)
    def _():
        g = arriving[...]
        for s in reversed(range(NY)):
            kept[s] = g
            if s == 0 and last:
                break
            dz = (dot(g, weights[s, 1], 1, 1) * slopes[s]).astype(jnp.bfloat16)
            g = (g.astype(jnp.float32) + dot(dz, weights[s, 0], 1, 1)).astype(jnp.bfloat16)
        if not last:
            sending[...] = g

    @pl.when(place[0] != NZ - 1 - tick)
    def _():
        kept[...] = kept_in[...]


def reduce_replicas(grads, zh, core):
    width = grads.shape[-1]
    rows = grads.shape[1] // (2 * NX * 2)
    parts = grads.reshape(2, 2, NX, 2, rows, width).transpose(2, 1, 0, 3, 4, 5)
    sent = lax.dynamic_index_in_dim(parts, 1 - core, 3, keepdims=False).astype(jnp.bfloat16)
    total = lax.dynamic_index_in_dim(parts, core, 3, keepdims=False)
    total = total + lax.ppermute(sent, "dp", replica_route(0, 1))
    total = over_x(total.astype(jnp.bfloat16)).astype(jnp.float32).sum(axis=0)
    sent = lax.dynamic_index_in_dim(total, 1 - zh, 0, keepdims=False).astype(jnp.bfloat16)
    own = lax.dynamic_index_in_dim(total, zh, 0, keepdims=False)
    return own + lax.ppermute(sent, "dp", replica_route(1, 0))


def body(section_inputs, cotangent, weight_in, weight_out):
    position = lax.axis_index("section")
    replica = lax.axis_index("dp")
    y = position % NY
    zh, core = replica // (2 * NX), replica % 2
    place = jnp.stack([position // NY, core]).astype(jnp.int32)
    micro, rows, width = section_inputs.shape[1:]
    shard = weight_in.shape[1]
    share = micro * rows // NY
    flat_x = section_inputs[0].reshape(micro * rows, width)

    own = jnp.concatenate([weight_in, weight_out], axis=0)
    other = lax.ppermute(own, "dp", replica_route(1, 0))
    both = jnp.where(zh == 0, jnp.stack([own, other]), jnp.stack([other, own]))
    lead = 4 * shard
    pieces = jnp.concatenate(
        [
            jnp.broadcast_to(both.reshape(1, lead, width), (NY, lead, width)),
            flat_x.reshape(NY, share, width),
        ],
        axis=1,
    )
    arrived = over_y(pieces)
    mine = over_x(jnp.broadcast_to(arrived[:, :lead].reshape(1, NY * lead, width), (NX, NY * lead, width)))
    mine = mine.reshape(NX, NY, 2, 2, shard, width)
    other = lax.ppermute(mine, "dp", replica_route(0, 1))
    weights, slopes = call(
        functools.partial(prepare_kernel, lead),
        (
            jax.ShapeDtypeStruct((NY, 2, width, width), jnp.bfloat16),
            jax.ShapeDtypeStruct((NY, share, width), jnp.float32),
        ),
        place,
        mine,
        other,
        arrived,
        flops=2 * NY * share * width * width,
    )

    arriving = lax.dynamic_index_in_dim(cotangent.reshape(NY, share, width), y, 0, keepdims=False)
    kept = jnp.zeros((NY, share, width), jnp.bfloat16)
    block = jax.ShapeDtypeStruct((share, width), jnp.bfloat16)
    home_at = NZ - 3
    for tick in range(NZ):
        kept, sending = call(
            functools.partial(stage_kernel, tick),
            (jax.ShapeDtypeStruct(kept.shape, kept.dtype), block),
            place,
            arriving,
            weights,
            slopes,
            kept,
            flops=4 * NY * share * width * width,
        )
        if tick == NZ - 1:
            break
        arriving = lax.ppermute(sending, "section", stage_route(NZ - 1 - tick))
        if tick == home_at:
            home_w = lax.dynamic_index_in_dim(weights, y, 0, keepdims=False)
            home_w, home_x, kept = lax.optimization_barrier((home_w, flat_x, kept))
            zed = dot(home_x, home_w[0], 1, 0)
            home_h = jax.nn.silu(zed).astype(jnp.bfloat16)
            home_slope = slope(zed)
            arriving, home_h, home_slope = lax.optimization_barrier((arriving, home_h, home_slope))

    home_g = over_y(kept).reshape(micro * rows, width)
    dz = (dot(home_g, home_w[1], 1, 1) * home_slope).astype(jnp.bfloat16)
    dx = (home_g.astype(jnp.float32) + dot(dz, home_w[0], 1, 1)).astype(jnp.bfloat16)
    grads = jnp.stack([dot(home_x, dz, 0, 0), RHO * dot(home_h, home_g, 0, 0)])
    factor = 4.0 / jnp.sqrt(jnp.float32(micro * rows * lax.axis_size("dp")))
    reduced = reduce_replicas(grads, zh, core) * factor
    return (reduced[0:1], reduced[1:2], dx.reshape(1, micro, rows, width))


def solution(mesh):
    return jax.shard_map(
        body,
        mesh=mesh,
        in_specs=(
            P("section", None, "dp", None),
            P(None, "dp", None),
            P("section", "dp", None),
            P("section", "dp", None),
        ),
        out_specs=(
            P("section", "dp", None),
            P("section", "dp", None),
            P("section", None, "dp", None),
        ),
        check_vma=False,
    )
```

```python
import functools

import jax
import jax.numpy as jnp
from jax import lax
from jax.experimental import pallas as pl
from jax.experimental.pallas import tpu as pltpu
from jax.sharding import Mesh
from jax.sharding import PartitionSpec as P

RHO = 0.25
NZ, NY, NH, NX, NC = 8, 4, 2, 4, 2
AXES = ("z_lo", "y", "z_hi", "x", "core")
PLANE = ("y", "x")
CHUNKS = 2
HOME_AT = NZ - 3
MIB = 1024 * 1024
BF16, F32 = jnp.bfloat16, jnp.float32
SWAP = [(0, 1), (1, 0)]


def struct(shape, dtype):
    return jax.ShapeDtypeStruct(shape, dtype)


def dot(left, right, left_dim, right_dim):
    return lax.dot_general(
        left, right, (((left_dim,), (right_dim,)), ((), ())), preferred_element_type=F32
    )


def slope(z):
    sig = 1.0 / (1.0 + jnp.exp(-z))
    return RHO * sig * (1.0 + z * (1.0 - sig))


def skip_first(kernel, _, *refs):
    kernel(*refs)


def call(kernel, out_shape, *operands, after=None, scratch=(), vmem=32, flops=0):
    whole = pl.BlockSpec(memory_space=pltpu.VMEM)
    specs = [
        pl.BlockSpec(memory_space=pltpu.SMEM) if o.dtype == jnp.int32 else whole for o in operands
    ]
    if after is not None:
        operands, specs = (after, *operands), [pl.BlockSpec(memory_space=pl.ANY), *specs]
        kernel = functools.partial(skip_first, kernel)
    return pl.pallas_call(
        kernel,
        out_shape=out_shape,
        in_specs=specs,
        out_specs=jax.tree.map(lambda _: whole, out_shape),
        scratch_shapes=list(scratch),
        cost_estimate=pl.CostEstimate(flops=flops, bytes_accessed=0, transcendentals=0),
        compiler_params=pltpu.CompilerParams(vmem_limit_bytes=vmem * MIB),
    )(*operands)


def prepare_kernel(place, mine, other, inputs, weights, slopes):
    rows = mine.shape[4]
    near_at = place[2] * (NX * NC * rows)
    far_at = NX * NC * rows - near_at
    mine_at = place[1] * rows
    other_at = rows - mine_at
    for s in reversed(range(NY)):
        for source, core_at in ((mine, mine_at), (other, other_at)):
            for half, half_at in enumerate((near_at, far_at)):
                for x in range(NX):
                    at = pl.multiple_of(half_at + x * NC * rows + core_at, rows)
                    for w in range(2):
                        weights[s, w, pl.ds(at, rows)] = source[s, x, half, w]
        slopes[s] = slope(dot(inputs[s], weights[s, 0], 1, 0))


def stage_kernel(stage, chunk, place, arriving, weights, slopes, kept_in, *rest):
    last = stage == NZ - 1
    joined = last and chunk == CHUNKS - 1
    earlier, outs = rest[: chunk if joined else 0], rest[chunk if joined else 0 :]
    part = arriving.shape[0]
    own = pl.ds(chunk * part, part)
    into = own if joined else pl.ds(0, part)
    for m, rows in enumerate(earlier):
        for s in range(NY):
            outs[0][s, pl.ds(m * part, part)] = rows[s]

    @pl.when(place[0] == NZ - 1 - stage)
    def _():
        g = arriving[...]
        for s in reversed(range(NY)):
            outs[0][s, into] = g
            if s == 0 and last:
                break
            dz = (dot(g, weights[s, 1], 1, 1) * slopes[s, own]).astype(BF16)
            g = (g.astype(F32) + dot(dz, weights[s, 0], 1, 1)).astype(BF16)
        if not last:
            outs[1][...] = g

    @pl.when(place[0] != NZ - 1 - stage)
    def _():
        for s in range(NY):
            outs[0][s, into] = kept_in[s]


def home_kernel(place, home_g, weights, slopes, inputs_t, h_t, dz, sent, own, grad):
    part = home_g.shape[0] // NY
    for block in range(NY):
        at = pl.ds(block * part, part)
        dz[at] = (dot(home_g[at], weights[1], 1, 1) * slopes[at]).astype(BF16)
    rows = sent.shape[3]
    for w, (left, right) in enumerate(((inputs_t, dz), (h_t, home_g))):
        product = dot(left[...], right[...], 1, 0)
        grad[...] = product * RHO if w else product
        for x in range(NX):
            for zh in range(NH):
                base = (zh * NX + x) * NC * rows
                at = pl.multiple_of(base + place[1] * rows, rows)
                own[x, zh, w] = grad[pl.ds(at, rows)]
                at = pl.multiple_of(base + (1 - place[1]) * rows, rows)
                sent[x, zh, w] = grad[pl.ds(at, rows)].astype(BF16)


def reduce_replicas(sent, own, zh):
    total = own + lax.ppermute(sent, "core", SWAP)
    total = lax.all_to_all(total.astype(BF16), "x", 0, 0).astype(F32).sum(axis=0)
    sent = lax.dynamic_index_in_dim(total, 1 - zh, 0, keepdims=False).astype(BF16)
    own = lax.dynamic_index_in_dim(total, zh, 0, keepdims=False)
    return own + lax.ppermute(sent, "z_hi", SWAP)


def body(section_inputs, cotangent, weight_in, weight_out):
    z, y, zh, _, core = (lax.axis_index(axis) for axis in AXES)
    place = jnp.stack([z, core, zh]).astype(jnp.int32)
    micro, rows, width = section_inputs.shape[1:]
    shard = weight_in.shape[1]
    share = micro * rows // NY
    part = share // CHUNKS
    flat_x = section_inputs.reshape(micro * rows, width)

    stage_x = lax.all_to_all(flat_x.reshape(NY, share, width), "y", 0, 0)
    own = jnp.concatenate([weight_in, weight_out], axis=0)
    far = lax.ppermute(own, "z_hi", SWAP)
    far, stage_x = lax.optimization_barrier((far, stage_x))
    block = jnp.concatenate([own, far], axis=0).reshape(1, 4 * shard, width)
    block = jnp.broadcast_to(block, (NY * NX, 4 * shard, width))
    mine = lax.all_to_all(block, PLANE, 0, 0).reshape(NY, NX, 2, 2, shard, width)
    other = lax.ppermute(mine, "core", SWAP)
    weights, slopes = call(
        prepare_kernel,
        (struct((NY, 2, width, width), BF16), struct((NY, share, width), F32)),
        place,
        mine,
        other,
        stage_x,
        flops=2 * NY * share * width * width,
    )

    given = lax.dynamic_index_in_dim(cotangent.reshape(NY, share, width), y, 0, keepdims=False)
    arriving = [given[m * part : (m + 1) * part] for m in range(CHUNKS)]
    kept = [jnp.zeros((NY, part, width), BF16) for _ in range(CHUNKS)]
    sending = None
    for stage in range(NZ):
        for m in range(CHUNKS):
            joined = stage == NZ - 1 and m == CHUNKS - 1
            outs = [struct((NY, share if joined else part, width), BF16)]
            if stage < NZ - 1:
                outs.append(struct((part, width), BF16))
            result = call(
                functools.partial(stage_kernel, stage, m),
                tuple(outs),
                place,
                arriving[m],
                weights,
                slopes,
                kept[m],
                *(kept[:m] if joined else ()),
                after=sending,
                flops=4 * NY * part * width * width,
            )
            kept[m] = result[0]
            if stage < NZ - 1:
                sending = result[1]
                arriving[m] = lax.ppermute(sending, "z_lo", [(NZ - 1 - stage, NZ - 2 - stage)])
        if stage == HOME_AT:
            home_w = lax.dynamic_index_in_dim(weights, y, 0, keepdims=False)
            home_w, home_x, _ = lax.optimization_barrier((home_w, flat_x, sending))
            home_slope = slope(dot(home_x, home_w[0], 1, 0))
            home_ht = jax.nn.silu(dot(home_w[0], home_x, 0, 1)).astype(BF16)
            home_xt = home_x.T
            arriving[0], home_slope, home_ht, home_xt, home_w = lax.optimization_barrier(
                (arriving[0], home_slope, home_ht, home_xt, home_w)
            )

    home_g = lax.all_to_all(kept[-1], "y", 0, 0).reshape(micro * rows, width)
    half = (NX, NH, 2, shard, width)
    dz, sent, own = call(
        home_kernel,
        (struct(home_g.shape, BF16), struct(half, BF16), struct(half, F32)),
        place,
        home_g,
        home_w,
        home_slope,
        home_xt,
        home_ht,
        scratch=[pltpu.VMEM((width, width), F32)],
        flops=6 * micro * rows * width * width,
    )
    dx = (home_g.astype(F32) + dot(dz, home_w[0], 1, 1)).astype(BF16)
    factor = 4.0 / jnp.sqrt(F32(micro * rows * NH * NX * NC))
    reduced = reduce_replicas(sent, own, zh) * factor
    return (reduced[0:1], reduced[1:2], dx.reshape(1, micro, rows, width))


def solution(mesh):
    named = Mesh(mesh.devices.reshape(NZ, NY, NH, NX, NC), AXES)
    section, dp = ("z_lo", "y"), ("z_hi", "x", "core")
    return jax.shard_map(
        body,
        mesh=named,
        in_specs=(
            P(section, None, dp, None),
            P(None, dp, None),
            P(section, dp, None),
            P(section, dp, None),
        ),
        out_specs=(
            P(section, dp, None),
            P(section, dp, None),
            P(section, None, dp, None),
        ),
        check_vma=False,
    )
```

```python
import functools

import jax
import jax.numpy as jnp
from jax import lax
from jax.experimental import pallas as pl
from jax.experimental.pallas import tpu as pltpu
from jax.sharding import Mesh
from jax.sharding import PartitionSpec as P

RHO = 0.25
NZ, NY, NH, NX, NC = 8, 4, 2, 4, 2
AXES = ("z_lo", "y", "z_hi", "x", "core")
PLANE = ("y", "x")
CHUNKS = 3
HOME_AT = NZ - 3
MIB = 1024 * 1024
BF16, F32 = jnp.bfloat16, jnp.float32
SWAP = [(0, 1), (1, 0)]


def struct(shape, dtype):
    return jax.ShapeDtypeStruct(shape, dtype)


def dot(left, right, left_dim, right_dim):
    return lax.dot_general(
        left, right, (((left_dim,), (right_dim,)), ((), ())), preferred_element_type=F32
    )


def slope(z):
    sig = 1.0 / (1.0 + jnp.exp(-z))
    return RHO * sig * (1.0 + z * (1.0 - sig))


def skip_first(kernel, _, *refs):
    kernel(*refs)


def call(kernel, out_shape, *operands, after=None, scratch=(), vmem=32, flops=0):
    whole = pl.BlockSpec(memory_space=pltpu.VMEM)
    specs = [
        pl.BlockSpec(memory_space=pltpu.SMEM) if o.dtype == jnp.int32 else whole for o in operands
    ]
    if after is not None:
        operands, specs = (after, *operands), [pl.BlockSpec(memory_space=pl.ANY), *specs]
        kernel = functools.partial(skip_first, kernel)
    return pl.pallas_call(
        kernel,
        out_shape=out_shape,
        in_specs=specs,
        out_specs=jax.tree.map(lambda _: whole, out_shape),
        scratch_shapes=list(scratch),
        cost_estimate=pl.CostEstimate(flops=flops, bytes_accessed=0, transcendentals=0),
        compiler_params=pltpu.CompilerParams(vmem_limit_bytes=vmem * MIB),
    )(*operands)


def prepare_kernel(place, mine, other, inputs, weights, slopes, natural):
    rows = mine.shape[4]
    near_at = place[2] * (NX * NC * rows)
    far_at = NX * NC * rows - near_at
    mine_at = place[1] * rows
    other_at = rows - mine_at
    for s in reversed(range(NY)):
        for source, core_at in ((mine, mine_at), (other, other_at)):
            for half, half_at in enumerate((near_at, far_at)):
                for x in range(NX):
                    at = pl.multiple_of(half_at + x * NC * rows + core_at, rows)
                    for w in range(2):
                        natural[s, w, pl.ds(at, rows)] = source[s, x, half, w]
        slopes[s] = slope(dot(inputs[s], natural[s, 0], 1, 0))
        for w in range(2):
            weights[s, w] = natural[s, w].T


def stage_kernel(stage, chunk, place, arriving, weights, slopes, kept_in, *rest):
    last = stage == NZ - 1
    joined = last and chunk == CHUNKS - 1
    earlier, outs = rest[: chunk if joined else 0], rest[chunk if joined else 0 :]
    part = arriving.shape[0]
    own = pl.ds(chunk * part, part)
    into = own if joined else pl.ds(0, part)
    for m, rows in enumerate(earlier):
        for s in range(NY):
            outs[0][s, pl.ds(m * part, part)] = rows[s]

    @pl.when(place[0] == NZ - 1 - stage)
    def _():
        g = arriving[...]
        for s in reversed(range(NY)):
            outs[0][s, into] = g
            if s == 0 and last:
                break
            dz = (dot(g, weights[s, 1], 1, 0) * slopes[s, own]).astype(BF16)
            g = (g.astype(F32) + dot(dz, weights[s, 0], 1, 0)).astype(BF16)
        if not last:
            outs[1][...] = g

    @pl.when(place[0] != NZ - 1 - stage)
    def _():
        for s in range(NY):
            outs[0][s, into] = kept_in[s]


def forward_kernel(place, inputs, weights, slopes, inputs_t, h_t):
    w_in = weights[place[3], 0]
    part = inputs.shape[0] // 3
    for block in range(3):
        at = pl.ds(block * part, part)
        x = inputs[at]
        zed = dot(x, w_in, 1, 1)
        sig = 1.0 / (1.0 + jnp.exp(-zed))
        slopes[at] = RHO * sig * (1.0 + zed * (1.0 - sig))
        h_t[:, at] = (zed * sig).astype(BF16).T
        inputs_t[:, at] = x.T


def add_kernel(own, arrived, total):
    total[...] = (own[...] + arrived[...].astype(F32)).astype(BF16)


def input_kernel(place, home_g, dz, weights, dx):
    w_in = weights[place[3], 0]
    part = home_g.shape[0] // NY
    for block in range(NY):
        at = pl.ds(block * part, part)
        dx[at] = (home_g[at].astype(F32) + dot(dz[at], w_in, 1, 0)).astype(BF16)


def home_kernel(place, home_g, weights, slopes, inputs_t, h_t, dz, sent, own, grad):
    w_out = weights[place[3], 1]
    part = home_g.shape[0] // NY
    for block in range(NY):
        at = pl.ds(block * part, part)
        dz[at] = (dot(home_g[at], w_out, 1, 0) * slopes[at]).astype(BF16)
    rows = sent.shape[3]
    for w, (left, right) in enumerate(((inputs_t, dz), (h_t, home_g))):
        product = dot(left[...], right[...], 1, 0)
        grad[...] = product * RHO if w else product
        for x in range(NX):
            for zh in range(NH):
                base = (zh * NX + x) * NC * rows
                at = pl.multiple_of(base + place[1] * rows, rows)
                own[x, zh, w] = grad[pl.ds(at, rows)]
                at = pl.multiple_of(base + (1 - place[1]) * rows, rows)
                sent[x, zh, w] = grad[pl.ds(at, rows)].astype(BF16)


def body(section_inputs, cotangent, weight_in, weight_out):
    z, y, zh, _, core = (lax.axis_index(axis) for axis in AXES)
    place = jnp.stack([z, core, zh, y]).astype(jnp.int32)
    micro, rows, width = section_inputs.shape[1:]
    shard = weight_in.shape[1]
    share = micro * rows // NY
    part = share // CHUNKS
    flat_x = section_inputs.reshape(micro * rows, width)

    stage_x = lax.all_to_all(flat_x.reshape(NY, share, width), "y", 0, 0)
    own = jnp.concatenate([weight_in, weight_out], axis=0)
    far = lax.ppermute(own, "z_hi", SWAP)
    given = lax.dynamic_index_in_dim(cotangent.reshape(NY, share, width), y, 0, keepdims=False)
    arriving = [given[m * part : (m + 1) * part] for m in range(CHUNKS)]
    far, stage_x, *arriving = lax.optimization_barrier((far, stage_x, *arriving))
    block = jnp.concatenate([own, far], axis=0).reshape(1, 4 * shard, width)
    block = jnp.broadcast_to(block, (NY * NX, 4 * shard, width))
    mine = lax.all_to_all(block, PLANE, 0, 0).reshape(NY, NX, 2, 2, shard, width)
    other = lax.ppermute(mine, "core", SWAP)
    weights, slopes = call(
        prepare_kernel,
        (struct((NY, 2, width, width), BF16), struct((NY, share, width), F32)),
        place,
        mine,
        other,
        stage_x,
        scratch=[pltpu.VMEM((NY, 2, width, width), BF16)],
        flops=2 * NY * share * width * width,
    )

    kept = [jnp.zeros((NY, part, width), BF16) for _ in range(CHUNKS)]
    sending = None
    for stage in range(NZ):
        for m in range(CHUNKS):
            joined = stage == NZ - 1 and m == CHUNKS - 1
            outs = [struct((NY, share if joined else part, width), BF16)]
            if stage < NZ - 1:
                outs.append(struct((part, width), BF16))
            result = call(
                functools.partial(stage_kernel, stage, m),
                tuple(outs),
                place,
                arriving[m],
                weights,
                slopes,
                kept[m],
                *(kept[:m] if joined else ()),
                after=sending,
                flops=4 * NY * part * width * width,
            )
            kept[m], sending = result[0], result[-1]
            if stage < NZ - 1:
                arriving[m] = lax.ppermute(sending, "z_lo", [(NZ - 1 - stage, NZ - 2 - stage)])
        if stage == HOME_AT:
            wide = struct((width, micro * rows), BF16)
            home = call(
                forward_kernel,
                (struct(flat_x.shape, F32), wide, wide),
                place,
                flat_x,
                weights,
                after=sending,
                flops=2 * micro * rows * width * width,
            )
            arriving[0], *home = lax.optimization_barrier((arriving[0], *home))

    home_g = lax.all_to_all(kept[-1], "y", 0, 0).reshape(micro * rows, width)
    half = (NX, NH, 2, shard, width)
    dz, sent, own = call(
        home_kernel,
        (struct(home_g.shape, BF16), struct(half, BF16), struct(half, F32)),
        place,
        home_g,
        weights,
        *home,
        scratch=[pltpu.VMEM((width, width), F32)],
        flops=6 * micro * rows * width * width,
    )
    (total,) = call(add_kernel, (struct(half, BF16),), own, lax.ppermute(sent, "core", SWAP))
    parts = lax.all_to_all(total, "x", 0, 0)
    (dx,) = call(
        input_kernel,
        (struct(home_g.shape, BF16),),
        place,
        home_g,
        dz,
        weights,
        after=parts,
        flops=2 * micro * rows * width * width,
    )
    total = parts.astype(F32).sum(axis=0)
    sent = lax.dynamic_index_in_dim(total, 1 - zh, 0, keepdims=False).astype(BF16)
    own = lax.dynamic_index_in_dim(total, zh, 0, keepdims=False)
    factor = 4.0 / jnp.sqrt(F32(micro * rows * NH * NX * NC))
    reduced = (own + lax.ppermute(sent, "z_hi", SWAP)) * factor
    return (reduced[0:1], reduced[1:2], dx.reshape(1, micro, rows, width))


def solution(mesh):
    named = Mesh(mesh.devices.reshape(NZ, NY, NH, NX, NC), AXES)
    section, dp = ("z_lo", "y"), ("z_hi", "x", "core")
    return jax.shard_map(
        body,
        mesh=named,
        in_specs=(
            P(section, None, dp, None),
            P(None, dp, None),
            P(section, dp, None),
            P(section, dp, None),
        ),
        out_specs=(
            P(section, dp, None),
            P(section, dp, None),
            P(section, None, dp, None),
        ),
        check_vma=False,
    )
```

```python
import functools
import math

import jax
import jax.numpy as jnp
from jax import lax
from jax.experimental import pallas as pl
from jax.experimental.pallas import tpu as pltpu
from jax.sharding import Mesh
from jax.sharding import PartitionSpec as P

RHO = 0.25
NZ, NY, NH, NX, NC = 8, 4, 2, 4, 2
AXES = ("z_lo", "y", "z_hi", "x", "core")
PLANE = ("y", "x")
CHUNKS = 3
HOME_AT = NZ - 3
MIB = 1024 * 1024
BF16, F32 = jnp.bfloat16, jnp.float32
SWAP = [(0, 1), (1, 0)]


def struct(shape, dtype):
    return jax.ShapeDtypeStruct(shape, dtype)


def dot(left, right, left_dim, right_dim):
    return lax.dot_general(
        left, right, (((left_dim,), (right_dim,)), ((), ())), preferred_element_type=F32
    )


def slope(z):
    sig = 1.0 / (1.0 + jnp.exp(-z))
    return RHO * sig * (1.0 + z * (1.0 - sig))


def skip_first(kernel, _, *refs):
    kernel(*refs)


def call(kernel, out_shape, *operands, after=None, scratch=(), vmem=32, flops=0):
    whole = pl.BlockSpec(memory_space=pltpu.VMEM)
    specs = [
        pl.BlockSpec(memory_space=pltpu.SMEM) if o.dtype == jnp.int32 else whole for o in operands
    ]
    if after is not None:
        operands, specs = (after, *operands), [pl.BlockSpec(memory_space=pl.ANY), *specs]
        kernel = functools.partial(skip_first, kernel)
    return pl.pallas_call(
        kernel,
        out_shape=out_shape,
        in_specs=specs,
        out_specs=jax.tree.map(lambda _: whole, out_shape),
        scratch_shapes=list(scratch),
        cost_estimate=pl.CostEstimate(flops=flops, bytes_accessed=0, transcendentals=0),
        compiler_params=pltpu.CompilerParams(vmem_limit_bytes=vmem * MIB),
    )(*operands)


def prepare_kernel(place, mine, other, inputs, weights, slopes, natural):
    rows = mine.shape[4]
    near_at = place[2] * (NX * NC * rows)
    far_at = NX * NC * rows - near_at
    mine_at = place[1] * rows
    other_at = rows - mine_at
    for s in reversed(range(NY)):
        for source, core_at in ((mine, mine_at), (other, other_at)):
            for half, half_at in enumerate((near_at, far_at)):
                for x in range(NX):
                    at = pl.multiple_of(half_at + x * NC * rows + core_at, rows)
                    for w in range(2):
                        natural[s, w, pl.ds(at, rows)] = source[s, x, half, w]
        slopes[s] = slope(dot(inputs[s], natural[s, 0], 1, 0))
        for w in range(2):
            weights[s, w] = natural[s, w].T


def stage_kernel(stage, chunk, place, arriving, weights, slopes, kept_in, *rest):
    last = stage == NZ - 1
    joined = last and chunk == CHUNKS - 1
    earlier, outs = rest[: chunk if joined else 0], rest[chunk if joined else 0 :]
    part = arriving.shape[0]
    own = pl.ds(chunk * part, part)
    into = own if joined else pl.ds(0, part)
    for m, rows in enumerate(earlier):
        for s in range(NY):
            outs[0][s, pl.ds(m * part, part)] = rows[s]

    @pl.when(place[0] == NZ - 1 - stage)
    def _():
        g = arriving[...]
        for s in reversed(range(NY)):
            outs[0][s, into] = g
            if s == 0 and last:
                break
            dz = (dot(g, weights[s, 1], 1, 0) * slopes[s, own]).astype(BF16)
            g = (g.astype(F32) + dot(dz, weights[s, 0], 1, 0)).astype(BF16)
        if not last:
            outs[1][...] = g

    @pl.when(place[0] != NZ - 1 - stage)
    def _():
        for s in range(NY):
            outs[0][s, into] = kept_in[s]


def forward_kernel(place, inputs, weights, slopes, inputs_t, h_t):
    w_in = weights[place[3], 0]
    part = inputs.shape[0] // 3
    for block in range(3):
        at = pl.ds(block * part, part)
        x = inputs[at]
        zed = dot(x, w_in, 1, 1)
        sig = 1.0 / (1.0 + jnp.exp(-zed))
        slopes[at] = RHO * sig * (1.0 + zed * (1.0 - sig))
        h_t[:, at] = (zed * sig).astype(BF16).T
        inputs_t[:, at] = x.T


def add_kernel(own, arrived, total):
    total[...] = (own[...] + arrived[...].astype(F32)).astype(BF16)


def split_kernel(factor, place, parts, sent, own):
    zh = place[2]
    own[...] = sum(parts[x, zh].astype(F32) for x in range(NX)) * factor
    sent[...] = (sum(parts[x, 1 - zh].astype(F32) for x in range(NX)) * factor).astype(BF16)


def input_kernel(place, home_g, dz, weights, dx):
    w_in = weights[place[3], 0]
    part = home_g.shape[0] // NY
    for block in range(NY):
        at = pl.ds(block * part, part)
        dx[at] = (home_g[at].astype(F32) + dot(dz[at], w_in, 1, 0)).astype(BF16)


def home_kernel(place, home_g, weights, slopes, inputs_t, h_t, dz, sent, own, grad):
    w_out = weights[place[3], 1]
    part = home_g.shape[0] // NY
    for block in range(NY):
        at = pl.ds(block * part, part)
        dz[at] = (dot(home_g[at], w_out, 1, 0) * slopes[at]).astype(BF16)
    rows = sent.shape[3]
    for w, (left, right) in enumerate(((inputs_t, dz), (h_t, home_g))):
        product = dot(left[...], right[...], 1, 0)
        grad[...] = product * RHO if w else product
        for x in range(NX):
            for zh in range(NH):
                base = (zh * NX + x) * NC * rows
                at = pl.multiple_of(base + place[1] * rows, rows)
                own[x, zh, w] = grad[pl.ds(at, rows)]
                at = pl.multiple_of(base + (1 - place[1]) * rows, rows)
                sent[x, zh, w] = grad[pl.ds(at, rows)].astype(BF16)


def body(section_inputs, cotangent, weight_in, weight_out):
    z, y, zh, _, core = (lax.axis_index(axis) for axis in AXES)
    place = jnp.stack([z, core, zh, y]).astype(jnp.int32)
    micro, rows, width = section_inputs.shape[1:]
    shard = weight_in.shape[1]
    share = micro * rows // NY
    part = share // CHUNKS
    flat_x = section_inputs.reshape(micro * rows, width)

    stage_x = lax.all_to_all(flat_x.reshape(NY, share, width), "y", 0, 0)
    own = jnp.concatenate([weight_in, weight_out], axis=0)
    far = lax.ppermute(own, "z_hi", SWAP)
    given = lax.dynamic_index_in_dim(cotangent.reshape(NY, share, width), y, 0, keepdims=False)
    arriving = [given[m * part : (m + 1) * part] for m in range(CHUNKS)]
    far, stage_x, *arriving = lax.optimization_barrier((far, stage_x, *arriving))
    block = jnp.concatenate([own, far], axis=0).reshape(1, 4 * shard, width)
    block = jnp.broadcast_to(block, (NY * NX, 4 * shard, width))
    mine = lax.all_to_all(block, PLANE, 0, 0).reshape(NY, NX, 2, 2, shard, width)
    other = lax.ppermute(mine, "core", SWAP)
    weights, slopes = call(
        prepare_kernel,
        (struct((NY, 2, width, width), BF16), struct((NY, share, width), F32)),
        place,
        mine,
        other,
        stage_x,
        scratch=[pltpu.VMEM((NY, 2, width, width), BF16)],
        flops=2 * NY * share * width * width,
    )

    kept = [jnp.zeros((NY, part, width), BF16) for _ in range(CHUNKS)]
    sending = None
    for stage in range(NZ):
        for m in range(CHUNKS):
            joined = stage == NZ - 1 and m == CHUNKS - 1
            outs = [struct((NY, share if joined else part, width), BF16)]
            if stage < NZ - 1:
                outs.append(struct((part, width), BF16))
            result = call(
                functools.partial(stage_kernel, stage, m),
                tuple(outs),
                place,
                arriving[m],
                weights,
                slopes,
                kept[m],
                *(kept[:m] if joined else ()),
                after=sending,
                flops=4 * NY * part * width * width,
            )
            kept[m], sending = result[0], result[-1]
            if stage < NZ - 1:
                arriving[m] = lax.ppermute(sending, "z_lo", [(NZ - 1 - stage, NZ - 2 - stage)])
        if stage == HOME_AT:
            wide = struct((width, micro * rows), BF16)
            home = call(
                forward_kernel,
                (struct(flat_x.shape, F32), wide, wide),
                place,
                flat_x,
                weights,
                after=sending,
                flops=2 * micro * rows * width * width,
            )
            arriving[0], *home = lax.optimization_barrier((arriving[0], *home))

    home_g = lax.all_to_all(kept[-1], "y", 0, 0).reshape(micro * rows, width)
    half = (NX, NH, 2, shard, width)
    dz, sent, own = call(
        home_kernel,
        (struct(home_g.shape, BF16), struct(half, BF16), struct(half, F32)),
        place,
        home_g,
        weights,
        *home,
        scratch=[pltpu.VMEM((width, width), F32)],
        flops=6 * micro * rows * width * width,
    )
    (total,) = call(add_kernel, (struct(half, BF16),), own, lax.ppermute(sent, "core", SWAP))
    parts = lax.all_to_all(total, "x", 0, 0)
    factor = 4.0 / math.sqrt(micro * rows * NH * NX * NC)
    sent, own = call(
        functools.partial(split_kernel, factor),
        (struct((2, shard, width), BF16), struct((2, shard, width), F32)),
        place,
        parts,
    )
    (dx,) = call(
        input_kernel,
        (struct(home_g.shape, BF16),),
        place,
        home_g,
        dz,
        weights,
        after=sent,
        flops=2 * micro * rows * width * width,
    )
    reduced = own + lax.ppermute(sent, "z_hi", SWAP)
    return (reduced[0:1], reduced[1:2], dx.reshape(1, micro, rows, width))


def solution(mesh):
    named = Mesh(mesh.devices.reshape(NZ, NY, NH, NX, NC), AXES)
    section, dp = ("z_lo", "y"), ("z_hi", "x", "core")
    return jax.shard_map(
        body,
        mesh=named,
        in_specs=(
            P(section, None, dp, None),
            P(None, dp, None),
            P(section, dp, None),
            P(section, dp, None),
        ),
        out_specs=(
            P(section, dp, None),
            P(section, dp, None),
            P(section, None, dp, None),
        ),
        check_vma=False,
    )
```

```python
import functools
import math

import jax
import jax.numpy as jnp
from jax import lax
from jax.experimental import pallas as pl
from jax.experimental.pallas import tpu as pltpu
from jax.sharding import Mesh
from jax.sharding import PartitionSpec as P

RHO = 0.25
NZ, NY, NH, NX, NC = 8, 4, 2, 4, 2
AXES = ("z_lo", "y", "z_hi", "x", "core")
PLANE = ("y", "x", "core")
CHUNKS = 3
HOME_AT = NZ - 3
MIB = 1024 * 1024
BF16, F32 = jnp.bfloat16, jnp.float32
SWAP = [(0, 1), (1, 0)]


def plane_groups(first):
    def at(y, x, core):
        return (y * NX + x) * NC + core

    groups = []
    for core in range(NC):
        if (core == 0) == first:
            groups += [[at(y, x, core) for y in range(NY)] for x in range(NX)]
        else:
            groups += [[at(y, x, core) for x in range(NX)] for y in range(NY)]
    return groups


def gather_step(rows, first):
    pieces = jnp.broadcast_to(rows[None], (NY, *rows.shape))
    return lax.all_to_all(pieces, PLANE, 0, 0, axis_index_groups=plane_groups(first))


def struct(shape, dtype):
    return jax.ShapeDtypeStruct(shape, dtype)


def dot(left, right, left_dim, right_dim):
    return lax.dot_general(
        left, right, (((left_dim,), (right_dim,)), ((), ())), preferred_element_type=F32
    )


def slope(z):
    sig = 1.0 / (1.0 + jnp.exp(-z))
    return RHO * sig * (1.0 + z * (1.0 - sig))


def skip_first(kernel, _, *refs):
    kernel(*refs)


def call(kernel, out_shape, *operands, after=None, scratch=(), vmem=32, flops=0):
    whole = pl.BlockSpec(memory_space=pltpu.VMEM)
    specs = [
        pl.BlockSpec(memory_space=pltpu.SMEM) if o.dtype == jnp.int32 else whole for o in operands
    ]
    if after is not None:
        operands, specs = (after, *operands), [pl.BlockSpec(memory_space=pl.ANY), *specs]
        kernel = functools.partial(skip_first, kernel)
    return pl.pallas_call(
        kernel,
        out_shape=out_shape,
        in_specs=specs,
        out_specs=jax.tree.map(lambda _: whole, out_shape),
        scratch_shapes=list(scratch),
        cost_estimate=pl.CostEstimate(flops=flops, bytes_accessed=0, transcendentals=0),
        compiler_params=pltpu.CompilerParams(vmem_limit_bytes=vmem * MIB),
    )(*operands)


def prepare_kernel(place, mine, other, inputs, weights, slopes, natural):
    rows = mine.shape[3]
    core = place[1]
    near_at = place[2] * (NX * NC * rows)
    far_at = NX * NC * rows - near_at
    mine_at = place[1] * rows
    other_at = rows - mine_at
    for s in reversed(range(NY)):
        for source, core_at, c in ((mine, mine_at, core), (other, other_at, 1 - core)):
            for half, half_at in enumerate((near_at, far_at)):
                for x in range(NX):
                    at = pl.multiple_of(half_at + x * NC * rows + core_at, rows)
                    entry = (1 - c) * (x * NY + s) + c * (s * NX + x)
                    for w in range(2):
                        natural[s, w, pl.ds(at, rows)] = source[entry, half, w]
        slopes[s] = slope(dot(inputs[s], natural[s, 0], 1, 0))
        for w in range(2):
            weights[s, w] = natural[s, w].T


def stage_kernel(stage, chunk, place, arriving, weights, slopes, kept_in, *rest):
    last = stage == NZ - 1
    joined = last and chunk == CHUNKS - 1
    earlier, outs = rest[: chunk if joined else 0], rest[chunk if joined else 0 :]
    part = arriving.shape[0]
    own = pl.ds(chunk * part, part)
    into = own if joined else pl.ds(0, part)
    for m, rows in enumerate(earlier):
        for s in range(NY):
            outs[0][s, pl.ds(m * part, part)] = rows[s]

    @pl.when(place[0] == NZ - 1 - stage)
    def _():
        g = arriving[...]
        for s in reversed(range(NY)):
            outs[0][s, into] = g
            if s == 0 and last:
                break
            dz = (dot(g, weights[s, 1], 1, 0) * slopes[s, own]).astype(BF16)
            g = (g.astype(F32) + dot(dz, weights[s, 0], 1, 0)).astype(BF16)
        if not last:
            outs[1][...] = g

    @pl.when(place[0] != NZ - 1 - stage)
    def _():
        for s in range(NY):
            outs[0][s, into] = kept_in[s]


def forward_kernel(place, inputs, weights, slopes, inputs_t, h_t):
    w_in = weights[place[3], 0]
    part = inputs.shape[0] // 3
    for block in range(3):
        at = pl.ds(block * part, part)
        x = inputs[at]
        zed = dot(x, w_in, 1, 1)
        sig = 1.0 / (1.0 + jnp.exp(-zed))
        slopes[at] = RHO * sig * (1.0 + zed * (1.0 - sig))
        h_t[:, at] = (zed * sig).astype(BF16).T
        inputs_t[:, at] = x.T


def add_kernel(own, arrived, total):
    total[...] = (own[...] + arrived[...].astype(F32)).astype(BF16)


def split_kernel(factor, place, parts, sent, own):
    zh = place[2]
    own[...] = sum(parts[x, zh].astype(F32) for x in range(NX)) * factor
    sent[...] = (sum(parts[x, 1 - zh].astype(F32) for x in range(NX)) * factor).astype(BF16)


def input_kernel(place, home_g, dz, weights, dx):
    w_in = weights[place[3], 0]
    part = home_g.shape[0] // NY
    for block in range(NY):
        at = pl.ds(block * part, part)
        dx[at] = (home_g[at].astype(F32) + dot(dz[at], w_in, 1, 0)).astype(BF16)


def home_kernel(place, home_g, weights, slopes, inputs_t, h_t, dz, sent, own, grad):
    w_out = weights[place[3], 1]
    part = home_g.shape[0] // NY
    for block in range(NY):
        at = pl.ds(block * part, part)
        dz[at] = (dot(home_g[at], w_out, 1, 0) * slopes[at]).astype(BF16)
    rows = sent.shape[3]
    for w, (left, right) in enumerate(((inputs_t, dz), (h_t, home_g))):
        product = dot(left[...], right[...], 1, 0)
        grad[...] = product * RHO if w else product
        for x in range(NX):
            for zh in range(NH):
                base = (zh * NX + x) * NC * rows
                at = pl.multiple_of(base + place[1] * rows, rows)
                own[x, zh, w] = grad[pl.ds(at, rows)]
                at = pl.multiple_of(base + (1 - place[1]) * rows, rows)
                sent[x, zh, w] = grad[pl.ds(at, rows)].astype(BF16)


def body(section_inputs, cotangent, weight_in, weight_out):
    z, y, zh, _, core = (lax.axis_index(axis) for axis in AXES)
    place = jnp.stack([z, core, zh, y]).astype(jnp.int32)
    micro, rows, width = section_inputs.shape[1:]
    shard = weight_in.shape[1]
    share = micro * rows // NY
    part = share // CHUNKS
    flat_x = section_inputs.reshape(micro * rows, width)

    stage_x = lax.all_to_all(flat_x.reshape(NY, share, width), "y", 0, 0)
    own = jnp.concatenate([weight_in, weight_out], axis=0)
    far = lax.ppermute(own, "z_hi", SWAP)
    given = lax.dynamic_index_in_dim(cotangent.reshape(NY, share, width), y, 0, keepdims=False)
    arriving = [given[m * part : (m + 1) * part] for m in range(CHUNKS)]
    far, stage_x, *arriving = lax.optimization_barrier((far, stage_x, *arriving))
    block = jnp.concatenate([own, far], axis=0).reshape(4 * shard, width)
    block = gather_step(block, True).reshape(NY * 4 * shard, width)
    mine = gather_step(block, False).reshape(NY * NX, 2, 2, shard, width)
    other = lax.ppermute(mine, "core", SWAP)
    weights, slopes = call(
        prepare_kernel,
        (struct((NY, 2, width, width), BF16), struct((NY, share, width), F32)),
        place,
        mine,
        other,
        stage_x,
        scratch=[pltpu.VMEM((NY, 2, width, width), BF16)],
        flops=2 * NY * share * width * width,
    )

    kept = [jnp.zeros((NY, part, width), BF16) for _ in range(CHUNKS)]
    sending = None
    for stage in range(NZ):
        for m in range(CHUNKS):
            joined = stage == NZ - 1 and m == CHUNKS - 1
            outs = [struct((NY, share if joined else part, width), BF16)]
            if stage < NZ - 1:
                outs.append(struct((part, width), BF16))
            result = call(
                functools.partial(stage_kernel, stage, m),
                tuple(outs),
                place,
                arriving[m],
                weights,
                slopes,
                kept[m],
                *(kept[:m] if joined else ()),
                after=sending,
                flops=4 * NY * part * width * width,
            )
            kept[m], sending = result[0], result[-1]
            if stage < NZ - 1:
                arriving[m] = lax.ppermute(sending, "z_lo", [(NZ - 1 - stage, NZ - 2 - stage)])
        if stage == HOME_AT:
            wide = struct((width, micro * rows), BF16)
            home = call(
                forward_kernel,
                (struct(flat_x.shape, F32), wide, wide),
                place,
                flat_x,
                weights,
                after=sending,
                flops=2 * micro * rows * width * width,
            )
            arriving[0], *home = lax.optimization_barrier((arriving[0], *home))

    home_g = lax.all_to_all(kept[-1], "y", 0, 0).reshape(micro * rows, width)
    half = (NX, NH, 2, shard, width)
    dz, sent, own = call(
        home_kernel,
        (struct(home_g.shape, BF16), struct(half, BF16), struct(half, F32)),
        place,
        home_g,
        weights,
        *home,
        scratch=[pltpu.VMEM((width, width), F32)],
        flops=6 * micro * rows * width * width,
    )
    (total,) = call(add_kernel, (struct(half, BF16),), own, lax.ppermute(sent, "core", SWAP))
    parts = lax.all_to_all(total, "x", 0, 0)
    factor = 4.0 / math.sqrt(micro * rows * NH * NX * NC)
    sent, own = call(
        functools.partial(split_kernel, factor),
        (struct((2, shard, width), BF16), struct((2, shard, width), F32)),
        place,
        parts,
    )
    (dx,) = call(
        input_kernel,
        (struct(home_g.shape, BF16),),
        place,
        home_g,
        dz,
        weights,
        after=sent,
        flops=2 * micro * rows * width * width,
    )
    reduced = own + lax.ppermute(sent, "z_hi", SWAP)
    return (reduced[0:1], reduced[1:2], dx.reshape(1, micro, rows, width))


def solution(mesh):
    named = Mesh(mesh.devices.reshape(NZ, NY, NH, NX, NC), AXES)
    section, dp = ("z_lo", "y"), ("z_hi", "x", "core")
    return jax.shard_map(
        body,
        mesh=named,
        in_specs=(
            P(section, None, dp, None),
            P(None, dp, None),
            P(section, dp, None),
            P(section, dp, None),
        ),
        out_specs=(
            P(section, dp, None),
            P(section, dp, None),
            P(section, None, dp, None),
        ),
        check_vma=False,
    )
```

```python
import functools
import math

import jax
import jax.numpy as jnp
from jax import lax
from jax.experimental import pallas as pl
from jax.experimental.pallas import tpu as pltpu
from jax.sharding import Mesh
from jax.sharding import PartitionSpec as P

RHO = 0.25
NZ, NY, NH, NX, NC = 8, 4, 2, 4, 2
AXES = ("z_lo", "y", "z_hi", "x", "core")
PLANE = ("y", "x", "core")
CHUNKS = 3
HOME_AT = NZ - 3
MIB = 1024 * 1024
BF16, F32 = jnp.bfloat16, jnp.float32
SWAP = [(0, 1), (1, 0)]


def plane_groups(first):
    def at(y, x, core):
        return (y * NX + x) * NC + core

    groups = []
    for core in range(NC):
        if (core == 0) == first:
            groups += [[at(y, x, core) for y in range(NY)] for x in range(NX)]
        else:
            groups += [[at(y, x, core) for x in range(NX)] for y in range(NY)]
    return groups


def gather_step(rows, first):
    pieces = jnp.broadcast_to(rows[None], (NY, *rows.shape))
    return lax.all_to_all(pieces, PLANE, 0, 0, axis_index_groups=plane_groups(first))


def struct(shape, dtype):
    return jax.ShapeDtypeStruct(shape, dtype)


def dot(left, right, left_dim, right_dim):
    return lax.dot_general(
        left, right, (((left_dim,), (right_dim,)), ((), ())), preferred_element_type=F32
    )


def slope(z):
    sig = 1.0 / (1.0 + jnp.exp(-z))
    return RHO * sig * (1.0 + z * (1.0 - sig))


def skip_first(kernel, _, *refs):
    kernel(*refs)


def call(kernel, out_shape, *operands, after=None, scratch=(), vmem=32, flops=0):
    whole = pl.BlockSpec(memory_space=pltpu.VMEM)
    specs = [
        pl.BlockSpec(memory_space=pltpu.SMEM) if o.dtype == jnp.int32 else whole for o in operands
    ]
    if after is not None:
        operands, specs = (after, *operands), [pl.BlockSpec(memory_space=pl.ANY), *specs]
        kernel = functools.partial(skip_first, kernel)
    return pl.pallas_call(
        kernel,
        out_shape=out_shape,
        in_specs=specs,
        out_specs=jax.tree.map(lambda _: whole, out_shape),
        scratch_shapes=list(scratch),
        cost_estimate=pl.CostEstimate(flops=flops, bytes_accessed=0, transcendentals=0),
        compiler_params=pltpu.CompilerParams(vmem_limit_bytes=vmem * MIB),
    )(*operands)


def prepare_kernel(place, mine, other, inputs, weights, slopes, natural):
    rows = mine.shape[3]
    core = place[1]
    near_at = place[2] * (NX * NC * rows)
    far_at = NX * NC * rows - near_at
    mine_at = place[1] * rows
    other_at = rows - mine_at
    for s in reversed(range(NY)):
        for source, core_at, c in ((mine, mine_at, core), (other, other_at, 1 - core)):
            for half, half_at in enumerate((near_at, far_at)):
                for x in range(NX):
                    at = pl.multiple_of(half_at + x * NC * rows + core_at, rows)
                    entry = (1 - c) * (x * NY + s) + c * (s * NX + x)
                    for w in range(2):
                        natural[s, w, pl.ds(at, rows)] = source[entry, half, w]
        slopes[s] = slope(dot(inputs[s], natural[s, 0], 1, 0))
        for w in range(2):
            weights[s, w] = natural[s, w].T


def stage_kernel(stage, chunk, place, arriving, weights, slopes, kept_in, *rest):
    last = stage == NZ - 1
    joined = last and chunk == CHUNKS - 1
    earlier, outs = rest[: chunk if joined else 0], rest[chunk if joined else 0 :]
    part = arriving.shape[0]
    own = pl.ds(chunk * part, part)
    into = own if joined else pl.ds(0, part)
    for m, rows in enumerate(earlier):
        for s in range(NY):
            outs[0][s, pl.ds(m * part, part)] = rows[s]

    @pl.when(place[0] == NZ - 1 - stage)
    def _():
        g = arriving[...]
        for s in reversed(range(NY)):
            outs[0][s, into] = g
            if s == 0 and last:
                break
            dz = (dot(g, weights[s, 1], 1, 0) * slopes[s, own]).astype(BF16)
            g = (g.astype(F32) + dot(dz, weights[s, 0], 1, 0)).astype(BF16)
        if not last:
            outs[1][...] = g

    @pl.when(place[0] != NZ - 1 - stage)
    def _():
        for s in range(NY):
            outs[0][s, into] = kept_in[s]


def forward_kernel(place, inputs, weights, slopes, inputs_t, h_t):
    w_in = weights[place[3], 0]
    part = inputs.shape[0] // 3
    shard = inputs_t.shape[1] // (NH * NX)
    for block in range(3):
        at = pl.ds(block * part, part)
        x = inputs[at]
        zed = dot(x, w_in, 1, 1)
        sig = 1.0 / (1.0 + jnp.exp(-zed))
        slopes[at] = RHO * sig * (1.0 + zed * (1.0 - sig))
        for target, rows in ((h_t, (zed * sig).astype(BF16).T), (inputs_t, x.T)):
            for owner in range(NH * NX):
                for core in range(NC):
                    start = (owner * NC + core) * shard
                    target[core, pl.ds(owner * shard, shard), at] = rows[start : start + shard]


def write_rows(target, w, product):
    rows = target.shape[3]
    for zh in range(NH):
        for x in range(NX):
            start = (zh * NX + x) * rows
            target[x, zh, w] = product[start : start + rows].astype(target.dtype)


def sent_kernel(place, home_g, weights, slopes, inputs_t, h_t, dz, sent):
    w_out = weights[place[3], 1]
    part = home_g.shape[0] // NY
    for block in range(NY):
        at = pl.ds(block * part, part)
        dz[at] = (dot(home_g[at], w_out, 1, 0) * slopes[at]).astype(BF16)
    write_rows(sent, 0, dot(inputs_t[1 - place[1]], dz[...], 1, 0))
    write_rows(sent, 1, RHO * dot(h_t[1 - place[1]], home_g[...], 1, 0))


def own_kernel(place, home_g, dz, inputs_t, h_t, own):
    write_rows(own, 0, dot(inputs_t[place[1]], dz[...], 1, 0))
    write_rows(own, 1, RHO * dot(h_t[place[1]], home_g[...], 1, 0))


def add_kernel(own, arrived, total):
    total[...] = (own[...] + arrived[...].astype(F32)).astype(BF16)


def split_kernel(factor, place, parts, sent, own):
    zh = place[2]
    own[...] = sum(parts[x, zh].astype(F32) for x in range(NX)) * factor
    sent[...] = (sum(parts[x, 1 - zh].astype(F32) for x in range(NX)) * factor).astype(BF16)


def input_kernel(place, home_g, dz, weights, dx):
    w_in = weights[place[3], 0]
    part = home_g.shape[0] // NY
    for block in range(NY):
        at = pl.ds(block * part, part)
        dx[at] = (home_g[at].astype(F32) + dot(dz[at], w_in, 1, 0)).astype(BF16)


def home_kernel(place, home_g, weights, slopes, inputs_t, h_t, dz, sent, own, grad):
    w_out = weights[place[3], 1]
    part = home_g.shape[0] // NY
    for block in range(NY):
        at = pl.ds(block * part, part)
        dz[at] = (dot(home_g[at], w_out, 1, 0) * slopes[at]).astype(BF16)
    rows = sent.shape[3]
    for w, (left, right) in enumerate(((inputs_t, dz), (h_t, home_g))):
        product = dot(left[...], right[...], 1, 0)
        grad[...] = product * RHO if w else product
        for x in range(NX):
            for zh in range(NH):
                base = (zh * NX + x) * NC * rows
                at = pl.multiple_of(base + place[1] * rows, rows)
                own[x, zh, w] = grad[pl.ds(at, rows)]
                at = pl.multiple_of(base + (1 - place[1]) * rows, rows)
                sent[x, zh, w] = grad[pl.ds(at, rows)].astype(BF16)


def body(section_inputs, cotangent, weight_in, weight_out):
    z, y, zh, _, core = (lax.axis_index(axis) for axis in AXES)
    place = jnp.stack([z, core, zh, y]).astype(jnp.int32)
    micro, rows, width = section_inputs.shape[1:]
    shard = weight_in.shape[1]
    share = micro * rows // NY
    part = share // CHUNKS
    flat_x = section_inputs.reshape(micro * rows, width)

    stage_x = lax.all_to_all(flat_x.reshape(NY, share, width), "y", 0, 0)
    own = jnp.concatenate([weight_in, weight_out], axis=0)
    far = lax.ppermute(own, "z_hi", SWAP)
    given = lax.dynamic_index_in_dim(cotangent.reshape(NY, share, width), y, 0, keepdims=False)
    arriving = [given[m * part : (m + 1) * part] for m in range(CHUNKS)]
    far, stage_x, *arriving = lax.optimization_barrier((far, stage_x, *arriving))
    block = jnp.concatenate([own, far], axis=0).reshape(4 * shard, width)
    block = gather_step(block, True).reshape(NY * 4 * shard, width)
    mine = gather_step(block, False).reshape(NY * NX, 2, 2, shard, width)
    other = lax.ppermute(mine, "core", SWAP)
    weights, slopes = call(
        prepare_kernel,
        (struct((NY, 2, width, width), BF16), struct((NY, share, width), F32)),
        place,
        mine,
        other,
        stage_x,
        scratch=[pltpu.VMEM((NY, 2, width, width), BF16)],
        flops=2 * NY * share * width * width,
    )

    kept = [jnp.zeros((NY, part, width), BF16) for _ in range(CHUNKS)]
    sending = None
    for stage in range(NZ):
        for m in range(CHUNKS):
            joined = stage == NZ - 1 and m == CHUNKS - 1
            outs = [struct((NY, share if joined else part, width), BF16)]
            if stage < NZ - 1:
                outs.append(struct((part, width), BF16))
            result = call(
                functools.partial(stage_kernel, stage, m),
                tuple(outs),
                place,
                arriving[m],
                weights,
                slopes,
                kept[m],
                *(kept[:m] if joined else ()),
                after=sending,
                flops=4 * NY * part * width * width,
            )
            kept[m], sending = result[0], result[-1]
            if stage < NZ - 1:
                arriving[m] = lax.ppermute(sending, "z_lo", [(NZ - 1 - stage, NZ - 2 - stage)])
        if stage == HOME_AT:
            wide = struct((NC, width // NC, micro * rows), BF16)
            home = call(
                forward_kernel,
                (struct(flat_x.shape, F32), wide, wide),
                place,
                flat_x,
                weights,
                after=sending,
                flops=2 * micro * rows * width * width,
            )
            arriving[0], *home = lax.optimization_barrier((arriving[0], *home))

    home_g = lax.all_to_all(kept[-1], "y", 0, 0).reshape(micro * rows, width)
    half = (NX, NH, 2, shard, width)
    home_slopes, *home_rows = home
    dz, sent = call(
        sent_kernel,
        (struct(home_g.shape, BF16), struct(half, BF16)),
        place,
        home_g,
        weights,
        home_slopes,
        *home_rows,
        flops=4 * micro * rows * width * width,
    )
    (own,) = call(
        own_kernel,
        (struct(half, F32),),
        place,
        home_g,
        dz,
        *home_rows,
        flops=2 * micro * rows * width * width,
    )
    (total,) = call(add_kernel, (struct(half, BF16),), own, lax.ppermute(sent, "core", SWAP))
    parts = lax.all_to_all(total, "x", 0, 0)
    factor = 4.0 / math.sqrt(micro * rows * NH * NX * NC)
    sent, own = call(
        functools.partial(split_kernel, factor),
        (struct((2, shard, width), BF16), struct((2, shard, width), F32)),
        place,
        parts,
    )
    (dx,) = call(
        input_kernel,
        (struct(home_g.shape, BF16),),
        place,
        home_g,
        dz,
        weights,
        after=sent,
        flops=2 * micro * rows * width * width,
    )
    reduced = own + lax.ppermute(sent, "z_hi", SWAP)
    return (reduced[0:1], reduced[1:2], dx.reshape(1, micro, rows, width))


def solution(mesh):
    named = Mesh(mesh.devices.reshape(NZ, NY, NH, NX, NC), AXES)
    section, dp = ("z_lo", "y"), ("z_hi", "x", "core")
    return jax.shard_map(
        body,
        mesh=named,
        in_specs=(
            P(section, None, dp, None),
            P(None, dp, None),
            P(section, dp, None),
            P(section, dp, None),
        ),
        out_specs=(
            P(section, dp, None),
            P(section, dp, None),
            P(section, None, dp, None),
        ),
        check_vma=False,
    )
```

```python
import functools
import math

import jax
import jax.numpy as jnp
from jax import lax
from jax.experimental import pallas as pl
from jax.experimental.pallas import tpu as pltpu
from jax.sharding import Mesh
from jax.sharding import PartitionSpec as P

RHO = 0.25
NZ, NY, NH, NX, NC = 8, 4, 2, 4, 2
AXES = ("z_lo", "y", "z_hi", "x", "core")
PLANE = ("y", "x", "core")
CHUNKS = 3
HOME_AT = NZ - 3
MIB = 1024 * 1024
BF16, F32 = jnp.bfloat16, jnp.float32
SWAP = [(0, 1), (1, 0)]


def plane_groups(first):
    def at(y, x, core):
        return (y * NX + x) * NC + core

    groups = []
    for core in range(NC):
        if (core == 0) == first:
            groups += [[at(y, x, core) for y in range(NY)] for x in range(NX)]
        else:
            groups += [[at(y, x, core) for x in range(NX)] for y in range(NY)]
    return groups


def gather_step(rows, first):
    pieces = jnp.broadcast_to(rows[None], (NY, *rows.shape))
    return lax.all_to_all(pieces, PLANE, 0, 0, axis_index_groups=plane_groups(first))


def struct(shape, dtype):
    return jax.ShapeDtypeStruct(shape, dtype)


def dot(left, right, left_dim, right_dim):
    return lax.dot_general(
        left, right, (((left_dim,), (right_dim,)), ((), ())), preferred_element_type=F32
    )


def slope(z):
    sig = 1.0 / (1.0 + jnp.exp(-z))
    return RHO * sig * (1.0 + z * (1.0 - sig))


def skip_first(kernel, _, *refs):
    kernel(*refs)


def call(kernel, out_shape, *operands, after=None, scratch=(), vmem=32, flops=0):
    whole = pl.BlockSpec(memory_space=pltpu.VMEM)
    specs = [
        pl.BlockSpec(memory_space=pltpu.SMEM) if o.dtype == jnp.int32 else whole for o in operands
    ]
    if after is not None:
        operands, specs = (after, *operands), [pl.BlockSpec(memory_space=pl.ANY), *specs]
        kernel = functools.partial(skip_first, kernel)
    return pl.pallas_call(
        kernel,
        out_shape=out_shape,
        in_specs=specs,
        out_specs=jax.tree.map(lambda _: whole, out_shape),
        scratch_shapes=list(scratch),
        cost_estimate=pl.CostEstimate(flops=flops, bytes_accessed=0, transcendentals=0),
        compiler_params=pltpu.CompilerParams(vmem_limit_bytes=vmem * MIB),
    )(*operands)


def prepare_kernel(place, mine, other, inputs, weights, slopes, natural):
    rows = mine.shape[3]
    core = place[1]
    near_at = place[2] * (NX * NC * rows)
    far_at = NX * NC * rows - near_at
    mine_at = place[1] * rows
    other_at = rows - mine_at
    for s in reversed(range(NY)):
        for source, core_at, c in ((mine, mine_at, core), (other, other_at, 1 - core)):
            for half, half_at in enumerate((near_at, far_at)):
                for x in range(NX):
                    at = pl.multiple_of(half_at + x * NC * rows + core_at, rows)
                    entry = (1 - c) * (x * NY + s) + c * (s * NX + x)
                    for w in range(2):
                        natural[s, w, pl.ds(at, rows)] = source[entry, half, w]
        slopes[s] = slope(dot(inputs[s], natural[s, 0], 1, 0))
        for w in range(2):
            weights[s, w] = natural[s, w].T


def stage_kernel(stage, chunk, arriving, weights, slopes, kept_in, *rest):
    last = stage == NZ - 1
    here = lax.axis_index("z_lo")
    joined = last and chunk == CHUNKS - 1
    earlier, outs = rest[: chunk if joined else 0], rest[chunk if joined else 0 :]
    part = arriving.shape[0]
    own = pl.ds(chunk * part, part)
    into = own if joined else pl.ds(0, part)
    for m, rows in enumerate(earlier):
        for s in range(NY):
            outs[0][s, pl.ds(m * part, part)] = rows[s]

    @pl.when(here == NZ - 1 - stage)
    def _():
        g = arriving[...]
        for s in reversed(range(NY)):
            outs[0][s, into] = g
            if s == 0 and last:
                break
            dz = (dot(g, weights[s, 1], 1, 0) * slopes[s, own]).astype(BF16)
            g = (g.astype(F32) + dot(dz, weights[s, 0], 1, 0)).astype(BF16)
        if not last:
            outs[1][...] = g

    @pl.when(here != NZ - 1 - stage)
    def _():
        for s in range(NY):
            outs[0][s, into] = kept_in[s]


def forward_kernel(place, inputs, weights, slopes, inputs_t, h_t):
    w_in = weights[place[3], 0]
    part = inputs.shape[0] // 3
    shard = inputs_t.shape[1] // (NH * NX)
    for block in range(3):
        at = pl.ds(block * part, part)
        x = inputs[at]
        zed = dot(x, w_in, 1, 1)
        sig = 1.0 / (1.0 + jnp.exp(-zed))
        slopes[at] = RHO * sig * (1.0 + zed * (1.0 - sig))
        for target, rows in ((h_t, (zed * sig).astype(BF16).T), (inputs_t, x.T)):
            for owner in range(NH * NX):
                for core in range(NC):
                    start = (owner * NC + core) * shard
                    target[core, pl.ds(owner * shard, shard), at] = rows[start : start + shard]


def write_rows(target, w, product):
    rows = target.shape[3]
    for zh in range(NH):
        for x in range(NX):
            start = (zh * NX + x) * rows
            target[x, zh, w] = product[start : start + rows].astype(target.dtype)


def sent_kernel(place, home_g, weights, slopes, inputs_t, h_t, dz, sent):
    w_out = weights[place[3], 1]
    part = home_g.shape[0] // NY
    for block in range(NY):
        at = pl.ds(block * part, part)
        dz[at] = (dot(home_g[at], w_out, 1, 0) * slopes[at]).astype(BF16)
    write_rows(sent, 0, dot(inputs_t[1 - place[1]], dz[...], 1, 0))
    write_rows(sent, 1, RHO * dot(h_t[1 - place[1]], home_g[...], 1, 0))


def own_kernel(place, home_g, dz, inputs_t, h_t, own):
    write_rows(own, 0, dot(inputs_t[place[1]], dz[...], 1, 0))
    write_rows(own, 1, RHO * dot(h_t[place[1]], home_g[...], 1, 0))


def add_kernel(own, arrived, total):
    total[...] = (own[...] + arrived[...].astype(F32)).astype(BF16)


def split_kernel(factor, place, parts, sent, own):
    zh = place[2]
    own[...] = sum(parts[x, zh].astype(F32) for x in range(NX)) * factor
    sent[...] = (sum(parts[x, 1 - zh].astype(F32) for x in range(NX)) * factor).astype(BF16)


def input_kernel(place, home_g, dz, weights, dx):
    w_in = weights[place[3], 0]
    part = home_g.shape[0] // NY
    for block in range(NY):
        at = pl.ds(block * part, part)
        dx[at] = (home_g[at].astype(F32) + dot(dz[at], w_in, 1, 0)).astype(BF16)


def home_kernel(place, home_g, weights, slopes, inputs_t, h_t, dz, sent, own, grad):
    w_out = weights[place[3], 1]
    part = home_g.shape[0] // NY
    for block in range(NY):
        at = pl.ds(block * part, part)
        dz[at] = (dot(home_g[at], w_out, 1, 0) * slopes[at]).astype(BF16)
    rows = sent.shape[3]
    for w, (left, right) in enumerate(((inputs_t, dz), (h_t, home_g))):
        product = dot(left[...], right[...], 1, 0)
        grad[...] = product * RHO if w else product
        for x in range(NX):
            for zh in range(NH):
                base = (zh * NX + x) * NC * rows
                at = pl.multiple_of(base + place[1] * rows, rows)
                own[x, zh, w] = grad[pl.ds(at, rows)]
                at = pl.multiple_of(base + (1 - place[1]) * rows, rows)
                sent[x, zh, w] = grad[pl.ds(at, rows)].astype(BF16)


def body(section_inputs, cotangent, weight_in, weight_out):
    z, y, zh, _, core = (lax.axis_index(axis) for axis in AXES)
    place = jnp.stack([z, core, zh, y]).astype(jnp.int32)
    micro, rows, width = section_inputs.shape[1:]
    shard = weight_in.shape[1]
    share = micro * rows // NY
    part = share // CHUNKS
    flat_x = section_inputs.reshape(micro * rows, width)

    stage_x = lax.all_to_all(flat_x.reshape(NY, share, width), "y", 0, 0)
    own = jnp.concatenate([weight_in, weight_out], axis=0)
    far = lax.ppermute(own, "z_hi", SWAP)
    given = lax.dynamic_index_in_dim(cotangent.reshape(NY, share, width), y, 0, keepdims=False)
    arriving = [given[m * part : (m + 1) * part] for m in range(CHUNKS)]
    far, stage_x, *arriving = lax.optimization_barrier((far, stage_x, *arriving))
    block = jnp.concatenate([own, far], axis=0).reshape(4 * shard, width)
    block = gather_step(block, True).reshape(NY * 4 * shard, width)
    mine = gather_step(block, False).reshape(NY * NX, 2, 2, shard, width)
    other = lax.ppermute(mine, "core", SWAP)
    weights, slopes = call(
        prepare_kernel,
        (struct((NY, 2, width, width), BF16), struct((NY, share, width), F32)),
        place,
        mine,
        other,
        stage_x,
        scratch=[pltpu.VMEM((NY, 2, width, width), BF16)],
        flops=2 * NY * share * width * width,
    )

    kept = [jnp.zeros((NY, part, width), BF16) for _ in range(CHUNKS)]
    sending = None
    for stage in range(NZ):
        for m in range(CHUNKS):
            joined = stage == NZ - 1 and m == CHUNKS - 1
            outs = [struct((NY, share if joined else part, width), BF16)]
            if stage < NZ - 1:
                outs.append(struct((part, width), BF16))
            result = call(
                functools.partial(stage_kernel, stage, m),
                tuple(outs),
                arriving[m],
                weights,
                slopes,
                kept[m],
                *(kept[:m] if joined else ()),
                after=sending,
                flops=4 * NY * part * width * width,
            )
            kept[m], sending = result[0], result[-1]
            if stage < NZ - 1:
                arriving[m] = lax.ppermute(sending, "z_lo", [(NZ - 1 - stage, NZ - 2 - stage)])
        if stage == HOME_AT:
            wide = struct((NC, width // NC, micro * rows), BF16)
            home = call(
                forward_kernel,
                (struct(flat_x.shape, F32), wide, wide),
                place,
                flat_x,
                weights,
                after=sending,
                flops=2 * micro * rows * width * width,
            )
            arriving[0], *home = lax.optimization_barrier((arriving[0], *home))

    home_g = lax.all_to_all(kept[-1], "y", 0, 0).reshape(micro * rows, width)
    half = (NX, NH, 2, shard, width)
    home_slopes, *home_rows = home
    dz, sent = call(
        sent_kernel,
        (struct(home_g.shape, BF16), struct(half, BF16)),
        place,
        home_g,
        weights,
        home_slopes,
        *home_rows,
        flops=4 * micro * rows * width * width,
    )
    (own,) = call(
        own_kernel,
        (struct(half, F32),),
        place,
        home_g,
        dz,
        *home_rows,
        flops=2 * micro * rows * width * width,
    )
    (total,) = call(add_kernel, (struct(half, BF16),), own, lax.ppermute(sent, "core", SWAP))
    parts = lax.all_to_all(total, "x", 0, 0)
    factor = 4.0 / math.sqrt(micro * rows * NH * NX * NC)
    sent, own = call(
        functools.partial(split_kernel, factor),
        (struct((2, shard, width), BF16), struct((2, shard, width), F32)),
        place,
        parts,
    )
    (dx,) = call(
        input_kernel,
        (struct(home_g.shape, BF16),),
        place,
        home_g,
        dz,
        weights,
        after=sent,
        flops=2 * micro * rows * width * width,
    )
    reduced = own + lax.ppermute(sent, "z_hi", SWAP)
    return (reduced[0:1], reduced[1:2], dx.reshape(1, micro, rows, width))


def solution(mesh):
    named = Mesh(mesh.devices.reshape(NZ, NY, NH, NX, NC), AXES)
    section, dp = ("z_lo", "y"), ("z_hi", "x", "core")
    return jax.shard_map(
        body,
        mesh=named,
        in_specs=(
            P(section, None, dp, None),
            P(None, dp, None),
            P(section, dp, None),
            P(section, dp, None),
        ),
        out_specs=(
            P(section, dp, None),
            P(section, dp, None),
            P(section, None, dp, None),
        ),
        check_vma=False,
    )
```
